256 devices in a mesh: outer: 32 (over z, x_lo, core), inner: 8 (over y, x_hi).
Axes of the slice: x: 4 (x_hi: 2, x_lo: 2; x = x_hi * 2 + x_lo), y: 4, z: 8, core: 2. Of those that a mesh axis runs over, the one named last changes fastest.
Arguments:
- inputs: bfloat16 [65536, 8192], P(('outer', 'inner')), may hold values from -24 to 24
- queries: bfloat16 [65536, 4096], P(('outer', 'inner')), may hold values from -120 to 120
- key_rows: bfloat16 [65536, 512], P(('outer', 'inner')), may hold values from -16 to 16
- out_grad: bfloat16 [65536, 4096], P(('outer', 'inner')), may hold values from -0.29882812 to 0.29882812
- sel_blocks: int32 [1024, 16], P(('outer', 'inner')), may hold values from 0 to 31, as said below
- block_mask: int32 [1024, 16], P(('outer', 'inner')), may hold values from 0 to 1
Outputs:
- weight_grad: float32 [8192, 512], P(('inner', 'outer'))
The draws below stay inside these ranges and needn't reach their ends.
Inputs may be any that keep to these rules, and one draw needn't show every extreme that they name: Row r of sel_blocks and block_mask belongs to query block r, at place b = r mod 32 in its sequence; the slots with block_mask 1 name distinct blocks numbered at most b, at most min(16, b + 1) of them, b itself always among them; slots with block_mask 0 may name any block of the sequence.
All inputs are finite; a program needn't handle non-finite values.
Results may differ from the reference program's by a relative error of at most 0.004.
Values may be sent and summed in bfloat16 or wider, within the bound.
A program may use at most 128 MiB of HBM per device.

```python
import math
import jax
import jax.numpy as jnp
from jax import lax

D = 8192
HD = 128
GROUP = 8
HK = 4
HQ = 32
BLK = 64
SEL = 16
SLAB = 2048
NB = 32
TOKENS = 65536
QBLOCKS = 1024
N_OUTER = 32


def pick_blocks(key):
    key = jax.random.fold_in(key, 101)
    width_all = max(NB, SEL)
    row_keys = jax.random.split(key, QBLOCKS)
    places = jnp.arange(QBLOCKS, dtype=jnp.int32) % NB

    def one_row(row_key, position):
        ranks = jax.random.permutation(jax.random.fold_in(row_key, 1), width_all).astype(jnp.int32)
        index = jnp.arange(width_all, dtype=jnp.int32)
        scores = jnp.where(index < position, ranks, -1 - index)
        scores = jnp.where(index == position, width_all, scores)
        _, chosen = lax.top_k(scores, SEL)
        chosen = chosen.astype(jnp.int32)
        usable = chosen <= position
        kept = jax.random.randint(jax.random.fold_in(row_key, 3), (SEL,), 0, 4, dtype=jnp.int32) != 0
        kept = kept | (chosen == position)
        filler = jax.random.randint(jax.random.fold_in(row_key, 2), (SEL,), 0, NB, dtype=jnp.int32)
        named = jnp.where(usable, chosen, filler).astype(jnp.int32)
        return (named, (usable & kept).astype(jnp.int32))
    return jax.vmap(one_row)(row_keys, places)


def base_keys(key):
    key = jax.random.fold_in(key, 202)
    return jnp.clip(jax.random.normal(key, (TOKENS, HK * HD), jnp.float32), -4.0, 4.0)


def draw_sel_blocks(key, part):
    chosen, usable = pick_blocks(key)
    return chosen


def draw_block_mask(key, part):
    chosen, usable = pick_blocks(key)
    return usable


def draw_key_rows(key, part):
    base = base_keys(key)
    return base.astype(jnp.bfloat16)


def draw_queries(key, part):
    key = jax.random.fold_in(key, 4)
    drawn = jnp.clip(jax.random.normal(key, (TOKENS, HQ * HD), jnp.float32), -4.0, 4.0)
    return drawn.astype(jnp.bfloat16)


def with_spikes(array, own_key, source, target, shards_of, factor):
    owner, partner = [(jnp.arange(array.shape[dim]) // (array.shape[dim] // shards_of)).reshape([-1 if axis == dim else 1 for axis in range(array.ndim)]) for dim in (source, target)]
    chosen = jax.random.permutation(own_key, shards_of)[partner]
    strong = (owner == chosen) | (owner == (partner + shards_of // 2) % shards_of)
    return jnp.where(strong, factor * array, array)


def level_of(rng, extent, shards, low, largest):
    factor_of = 1.0
    for axis_at, parts in shards:
        heights = jax.random.uniform(jax.random.fold_in(jax.random.fold_in(rng, 6), axis_at), (parts,), jnp.float32, low / len(shards), largest / len(shards))
        factor_of = factor_of * jnp.repeat(jnp.exp(heights), extent[axis_at] // parts).reshape((-1,) + (1,) * (len(extent) - 1 - axis_at))
    return factor_of


def centred(stream_key, dims, scale, bound, pieces=(), kind=jnp.bfloat16):
    loudness = level_of(stream_key, dims, pieces, -0.22, 0.18) if pieces else 1.0
    result = jax.random.normal(stream_key, dims, jnp.float32) * scale * loudness
    return jnp.minimum(jnp.maximum(result, -bound), bound).astype(kind)


def gaussian_with(stream_key, shape, width, most, pieces, heavy, kind=jnp.bfloat16):
    values = width * jax.random.normal(stream_key, shape, jnp.float32)
    if pieces:
        values = values * level_of(stream_key, shape, pieces, -0.22, 0.18)
    return jnp.clip(with_spikes(values, jax.random.fold_in(stream_key, 3), *heavy), -most, most).astype(kind)


def setup_inputs(seed: int = 0) -> dict:
    splits = jax.random.split(jax.random.key(seed), 7)
    return {
        "inputs": gaussian_with(splits[0], (TOKENS, D), 1.0, 24.0, ((0, 256),), (0, 1, 256, 6.0)),
        "queries": draw_queries(jax.random.fold_in(splits[6], 71), 0),
        "key_rows": draw_key_rows(jax.random.fold_in(splits[6], 71), 0),
        "out_grad": centred(splits[3], (TOKENS, HQ * HD), 0.05, 0.29882812, ((0, 256),)),
        "sel_blocks": draw_sel_blocks(jax.random.fold_in(splits[6], 71), 0),
        "block_mask": draw_block_mask(jax.random.fold_in(splits[6], 71), 0),
    }


def block_contrib(query_block, grad_block, sequence_keys, chosen, usable, position):
    query_heads = query_block.reshape(BLK, HK, GROUP, HD).astype(jnp.float32)
    picked = sequence_keys.reshape(NB, BLK, HK, HD)[chosen].reshape(SEL * BLK, HK, HD).astype(jnp.float32)
    factor = 1.0 / math.sqrt(HD)
    score = jnp.einsum('qgrd,ngd->grqn', query_heads, picked) * factor
    slot_of = jnp.arange(SEL * BLK, dtype=jnp.int32) // BLK
    within = jnp.arange(SEL * BLK, dtype=jnp.int32) % BLK
    block_of = chosen[slot_of]
    open_slot = usable[slot_of] == 1
    query_pos = jnp.arange(BLK, dtype=jnp.int32)[:, None]
    allowed = open_slot[None, :] & ((block_of[None, :] < position) | (block_of[None, :] == position) & (within[None, :] <= query_pos))
    masked = jnp.where(allowed[None, None], score, -1e+30)
    row_max = lax.optimization_barrier(jnp.max(masked, axis=-1, keepdims=True))
    weights = jnp.where(allowed[None, None], jnp.exp(masked - row_max), 0.0)
    probs = weights / lax.optimization_barrier(jnp.sum(weights, axis=-1, keepdims=True))
    probs = lax.optimization_barrier(probs.astype(jnp.bfloat16)).astype(jnp.float32)
    grad_heads = grad_block.reshape(BLK, HK, GROUP, HD).astype(jnp.float32)
    contrib = jnp.einsum('grqn,qgrd->ngd', probs, grad_heads)
    return contrib.reshape(SEL, BLK, HK * HD)

def reference(inputs, queries, key_rows, out_grad, sel_blocks, block_mask):
    query_all = queries.reshape(N_OUTER, NB, BLK, HQ * HD)
    grad_all = out_grad.reshape(N_OUTER, NB, BLK, HQ * HD)
    key_all = key_rows.reshape(N_OUTER, SLAB, HK * HD)
    chosen_all = sel_blocks.reshape(N_OUTER, NB, SEL)
    usable_all = block_mask.reshape(N_OUTER, NB, SEL)

    def one_sequence(packed):
        query_seq, grad_seq, key_seq, chosen_seq, usable_seq = packed

        def visit_block(running, block_item):
            query_block, grad_block, chosen, usable, position = block_item
            contrib = block_contrib(query_block, grad_block, key_seq, chosen, usable, position)
            return (running.at[chosen].add(contrib), None)
        start_value = jnp.zeros((NB, BLK, HK * HD), jnp.float32)
        places = jnp.arange(NB, dtype=jnp.int32)
        running, _ = lax.scan(visit_block, start_value, (query_seq, grad_seq, chosen_seq, usable_seq, places))
        return running
    value_grad = lax.map(one_sequence, (query_all, grad_all, key_all, chosen_all, usable_all))
    value_low = value_grad.reshape(TOKENS, HK * HD).astype(jnp.bfloat16)
    return lax.dot_general(inputs, value_low, (((0,), (0,)), ((), ())), preferred_element_type=jnp.float32)
```

```python
import math

import jax
import jax.numpy as jnp
from jax import lax
from jax.experimental import pallas as pl
from jax.experimental.pallas import tpu as pltpu
from jax.sharding import PartitionSpec as P

HD = 128
GROUP = 8
HK = 4
BLK = 64
SEL = 16
NB = 32
LB = 4
SCALE = math.log2(math.e) / math.sqrt(HD)
MESH = pl.DeviceIdType.MESH


def kernel(inputs, queries, key_rows, out_grad, sel, mask, out_ref, *scratch):
    scratch = list(scratch)

    def take(count):
        taken = scratch[:count]
        del scratch[:count]
        return taken

    keys = take(HK)
    give = take(HK)
    came = take(HK)
    value = take(HK)
    part = take(HK)
    part_in = take(HK)
    half = take(HK)
    half_in = take(HK)
    (q_ref, g_ref, x_ref, st_ref, contrib, bias, vacc, hacc, inverse) = take(9)
    (loc, key_s, key_r, x_s, x_r, give_s, give_r, val_s, val_r, p1_s, p1_r, p2_s, p2_r) = take(13)

    outer, inner = lax.axis_index("outer"), lax.axis_index("inner")
    core, xlo, z = lax.rem(outer, 2), lax.rem(outer // 2, 2), outer // 4
    y, xhi = inner // 2, lax.rem(inner, 2)
    slot = y * 2 + core

    def device(z_, xlo_, core_, y_, xhi_):
        return (z_ * 4 + xlo_ * 2 + core_, y_ * 2 + xhi_)

    def flip(value_, bit):
        return 1 - value_ if bit else value_

    def remote(src, dst, send, recv, target):
        return pltpu.make_async_remote_copy(
            src_ref=src, dst_ref=dst, send_sem=send, recv_sem=recv, device_id=target, device_id_type=MESH
        )

    q_loads = [
        pltpu.make_async_copy(
            queries.at[:, :, pl.ds(g * 1024, 1024)], q_ref.at[g], loc.at[0, g]
        )
        for g in range(HK)
    ]
    g_loads = [
        pltpu.make_async_copy(
            out_grad.at[:, :, pl.ds(g * 1024, 1024)], g_ref.at[g], loc.at[1, g]
        )
        for g in range(HK)
    ]
    k_loads = [
        pltpu.make_async_copy(
            key_rows.at[:, :, pl.ds(g * HD, HD)], keys[g].at[pl.ds(inner * LB, LB)], loc.at[2, g]
        )
        for g in range(HK)
    ]
    x_load = pltpu.make_async_copy(
        inputs.at[:, pl.ds(pl.multiple_of(slot * 1024, 1024), 1024)], x_ref.at[slot], loc.at[3, 0]
    )
    for g in range(HK):
        k_loads[g].start()
        q_loads[g].start()
        g_loads[g].start()

    barrier = pltpu.get_barrier_semaphore()

    def greet(target):
        pl.semaphore_signal(barrier, inc=1, device_id=target, device_id_type=MESH)

    for d in range(1, 8):
        greet((outer, lax.rem(inner + d, 8)))
    for dy in range(4):
        greet(device(z, xlo, 1 - core, lax.rem(y + dy, 4), xhi))
    for fl, fc, fh in ((0, 1, 1), (1, 0, 0), (1, 0, 1), (1, 1, 0), (1, 1, 1)):
        greet(device(z, flip(xlo, fl), flip(core, fc), y, flip(xhi, fh)))
    for d in range(1, 8):
        greet(device(lax.rem(z + d, 8), xlo, core, y, xhi))
    pl.semaphore_wait(barrier, 23)

    def key_copy(g, d):
        return remote(
            key_rows.at[:, :, pl.ds(g * HD, HD)],
            keys[g].at[pl.ds(inner * LB, LB)],
            key_s.at[g, d],
            key_r.at[g, d],
            (outer, lax.rem(inner + d, 8)),
        )

    def key_arrival(g, d):
        src = lax.rem(inner + 8 - d, 8)
        return remote(
            key_rows.at[:, :, pl.ds(g * HD, HD)],
            keys[g].at[pl.ds(src * LB, LB)],
            key_s.at[g, d],
            key_r.at[g, d],
            (outer, src),
        )

    for g in range(HK):
        for d in range(1, 8):

            @pl.when(inner + d < 8)
            def _():
                key_copy(g, d).start()

    spread = [(dy, dc) for dy in range(4) for dc in range(2) if (dy, dc) != (0, 0)]

    def peer(dy, dc):
        return lax.rem(y + dy, 4), flip(core, dc)

    def source(dy, dc):
        return lax.rem(y + 4 - dy, 4), flip(core, dc)

    def x_copy(dy, dc):
        py, pc = peer(dy, dc)
        return remote(
            inputs.at[:, pl.ds(pl.multiple_of((py * 2 + pc) * 1024, 1024), 1024)],
            x_ref.at[slot],
            x_s.at[dy * 2 + dc],
            x_r.at[dy * 2 + dc],
            device(z, xlo, pc, py, xhi),
        )

    def x_arrival(dy, dc):
        sy, sc = source(dy, dc)
        return remote(
            inputs.at[:, pl.ds(0, 1024)],
            x_ref.at[sy * 2 + sc],
            x_s.at[dy * 2 + dc],
            x_r.at[dy * 2 + dc],
            device(z, xlo, sc, sy, xhi),
        )

    x_load.start()
    for dy, dc in spread:
        x_copy(dy, dc).start()

    def invert(kb, carry):
        for qb in range(LB):
            found = jnp.int32(SEL)
            for s in range(SEL):
                found = jnp.where((mask[qb, s] == 1) & (sel[qb, s] == kb), jnp.int32(s), found)
            inverse[qb, kb] = found
        return carry

    lax.fori_loop(0, inner * LB + LB, invert, 0)
    key_at = lax.broadcasted_iota(jnp.int32, (BLK, HD), 0)
    query_at = lax.rem(lax.broadcasted_iota(jnp.int32, (BLK, HD), 1), BLK)
    bias[0] = jnp.zeros((BLK, HD), jnp.float32)
    bias[1] = jnp.where(key_at <= query_at, 0.0, -1e30).astype(jnp.float32)
    bias[2] = jnp.full((BLK, HD), -1e30, jnp.float32)
    for qb in range(LB):
        contrib[qb, SEL] = jnp.zeros((BLK, HD), jnp.float32)

    def heads(ref, g, qb):
        return jnp.concatenate([ref[g, qb, :, pl.ds(h * HD, HD)] for h in range(GROUP)], axis=0)

    def attend(g):
        def one(qb, carry):
            place = inner * LB + qb
            query = heads(q_ref, g, qb)
            top = jnp.full((8, GROUP * BLK), -3e38, jnp.float32)
            for quad in range(4):
                picked, masks = [], []
                for s in range(4 * quad, 4 * quad + 4):
                    used = mask[qb, s] == 1
                    block = sel[qb, s]
                    picked.append(keys[g][jnp.where(used, block, place)])
                    kind = jnp.where(used, jnp.where(block == place, 1, 0), 2)
                    masks.append(bias[kind])
                scores = lax.dot_general(
                    jnp.concatenate(picked, axis=0),
                    query,
                    (((1,), (1,)), ((), ())),
                    preferred_element_type=jnp.float32,
                )
                shift = jnp.concatenate(masks, axis=0)
                scores = scores + jnp.concatenate([shift] * 4, axis=1)
                st_ref[quad] = scores
                top = jnp.maximum(top, jnp.max(scores.reshape(32, 8, GROUP * BLK), axis=0))
            top = jnp.max(top, axis=0, keepdims=True)
            total = jnp.zeros((8, GROUP * BLK), jnp.float32)
            for quad in range(4):
                weights = jnp.exp2((st_ref[quad] - top) * SCALE)
                st_ref[quad] = weights
                total = total + jnp.sum(weights.reshape(32, 8, GROUP * BLK), axis=0)
            norm = 1.0 / jnp.sum(total, axis=0, keepdims=True)
            grad = heads(g_ref, g, qb)
            for quad in range(4):
                probs = (st_ref[quad] * norm).astype(jnp.bfloat16)
                done = jnp.dot(probs, grad, preferred_element_type=jnp.float32)
                contrib[qb, pl.ds(4 * quad, 4)] = done.reshape(4, BLK, HD)
            return carry

        lax.fori_loop(0, LB, one, 0)

    def give_copy(g, j):
        d = inner - j
        return remote(
            give[g].at[j], came[g].at[d - 1], give_s.at[g, d], give_r.at[g, d], (outer, j)
        )

    def give_arrival(g, d):
        src = lax.rem(inner + d, 8)
        return remote(
            give[g].at[src], came[g].at[d - 1], give_s.at[g, d], give_r.at[g, d], (outer, src)
        )

    def hand_out(g):
        def owner(j, carry):
            for t in range(LB):
                terms = [contrib[qb, inverse[qb, j * LB + t]] for qb in range(LB)]
                give[g][j, t] = (terms[0] + terms[1]) + (terms[2] + terms[3])

            @pl.when(j < inner)
            def _():
                give_copy(g, j).start()

            return carry

        lax.fori_loop(0, inner + 1, owner, 0)

    def value_copy(g, dy, dc):
        py, pc = peer(dy, dc)
        return remote(
            value[g].at[slot],
            value[g].at[slot],
            val_s.at[g, dy * 2 + dc],
            val_r.at[g, dy * 2 + dc],
            device(z, xlo, pc, py, xhi),
        )

    def value_arrival(g, dy, dc):
        sy, sc = source(dy, dc)
        return remote(
            value[g].at[sy * 2 + sc],
            value[g].at[sy * 2 + sc],
            val_s.at[g, dy * 2 + dc],
            val_r.at[g, dy * 2 + dc],
            device(z, xlo, sc, sy, xhi),
        )

    def own(g):
        vacc[...] = give[g][inner]
        for d in range(1, 8):

            @pl.when(inner + d < 8)
            def _():
                give_arrival(g, d).wait_recv()
                vacc[...] += came[g][d - 1]

        value[g][slot] = vacc[...].reshape(LB * BLK, HD).astype(jnp.bfloat16)
        for dy, dc in spread:
            value_copy(g, dy, dc).start()

    def part_copy(g, fl, fc):
        k = flip(xlo, fl) * 2 + flip(core, fc)
        return remote(
            part[g].at[:, k],
            part_in[g].at[xhi * 2 + xlo],
            p1_s.at[g, fl * 2 + fc],
            p1_r.at[g, xhi * 2 + xlo],
            device(z, flip(xlo, fl), flip(core, fc), y, core),
        )

    def part_arrival(g, src_hi, src_lo):
        return remote(
            part[g].at[:, 0],
            part_in[g].at[src_hi * 2 + src_lo],
            p1_s.at[g, 0],
            p1_r.at[g, src_hi * 2 + src_lo],
            device(z, src_lo, xhi, y, src_hi),
        )

    def multiply(g):
        for dy, dc in spread:
            value_arrival(g, dy, dc).wait_recv()
        low = value[g][...].reshape(8 * LB * BLK, HD)
        for tile in range(4):
            wide = x_ref[:, :, pl.ds(tile * 256, 256)].reshape(8 * LB * BLK, 256)
            term = lax.dot_general(
                low, wide, (((0,), (0,)), ((), ())), preferred_element_type=jnp.float32
            )
            part[g][pl.ds(2 * tile, 2)] = term.T.astype(jnp.bfloat16).reshape(2, 4, 32, HD)
        for fl in range(2):
            for fc in range(2):
                if (fl, fc) == (0, 0):

                    @pl.when(xhi != core)
                    def _():
                        part_copy(g, 0, 0).start()

                    @pl.when(xhi == core)
                    def _():
                        part_in[g][xhi * 2 + xlo] = part[g][:, xlo * 2 + core]

                else:
                    part_copy(g, fl, fc).start()

    def half_copy(g, d):
        to = lax.rem(z + d, 8)
        return remote(
            half[g].at[to],
            half_in[g].at[d - 1],
            p2_s.at[g, d],
            p2_r.at[g, d],
            device(to, xlo, core, y, xhi),
        )

    def half_arrival(g, d):
        src = lax.rem(z + 8 - d, 8)
        return remote(
            half[g].at[src],
            half_in[g].at[d - 1],
            p2_s.at[g, d],
            p2_r.at[g, d],
            device(src, xlo, core, y, xhi),
        )

    def shrink(g):
        for src_hi in range(2):
            for src_lo in range(2):

                @pl.when((src_hi != xhi) | (src_lo != xlo) | (core != xhi))
                def _():
                    part_arrival(g, src_hi, src_lo).wait_recv()

        terms = [part_in[g][k].astype(jnp.float32) for k in range(4)]
        hacc[g] = (terms[0] + terms[1]) + (terms[2] + terms[3])
        half[g][...] = hacc[g].astype(jnp.bfloat16)
        for d in range(1, 8):
            half_copy(g, d).start()

    def finish(g):
        total = hacc[g, z]
        for d in range(1, 8):
            half_arrival(g, d).wait_recv()
            total = total + half_in[g][d - 1].astype(jnp.float32)
        out_ref[:, pl.ds(g * HD, HD)] = total

    def start_of(g):
        k_loads[g].wait()
        q_loads[g].wait()
        g_loads[g].wait()
        for d in range(1, 8):

            @pl.when(inner - d >= 0)
            def _():
                key_arrival(g, d).wait_recv()

    start_of(0)
    attend(0)
    hand_out(0)
    start_of(1)
    attend(1)
    hand_out(1)
    own(0)
    start_of(2)
    attend(2)
    hand_out(2)
    own(1)
    start_of(3)
    attend(3)
    hand_out(3)
    own(2)
    x_load.wait()
    for dy, dc in spread:
        x_arrival(dy, dc).wait_recv()
    multiply(0)
    own(3)
    multiply(1)
    shrink(0)
    multiply(2)
    shrink(1)
    multiply(3)
    shrink(2)
    shrink(3)
    for g in range(HK):
        finish(g)

    for g in range(HK):
        for d in range(1, 8):

            @pl.when(inner + d < 8)
            def _():
                key_copy(g, d).wait_send()

            @pl.when(inner - d >= 0)
            def _():
                give_copy(g, inner - d).wait_send()

            half_copy(g, d).wait_send()
        for dy, dc in spread:
            value_copy(g, dy, dc).wait_send()
        for fl in range(2):
            for fc in range(2):
                if (fl, fc) == (0, 0):

                    @pl.when(xhi != core)
                    def _():
                        part_copy(g, 0, 0).wait_send()

                else:
                    part_copy(g, fl, fc).wait_send()
    for dy, dc in spread:
        x_copy(dy, dc).wait_send()


def body(inputs, queries, key_rows, out_grad, sel_blocks, block_mask):
    any_ref = pl.BlockSpec(memory_space=pl.ANY)
    smem = pl.BlockSpec(memory_space=pltpu.SMEM)
    bf16, f32 = jnp.bfloat16, jnp.float32
    dma = pltpu.SemaphoreType.DMA
    scratch = (
        [pltpu.VMEM((NB, BLK, HD), bf16)] * HK
        + [pltpu.VMEM((8, LB, BLK, HD), f32)] * HK
        + [pltpu.VMEM((7, LB, BLK, HD), f32)] * HK
        + [pltpu.VMEM((8, LB * BLK, HD), bf16)] * HK
        + [pltpu.VMEM((8, 4, 32, HD), bf16)] * HK
        + [pltpu.VMEM((4, 8, 32, HD), bf16)] * HK
        + [pltpu.VMEM((8, 32, HD), bf16)] * HK
        + [pltpu.VMEM((7, 32, HD), bf16)] * HK
        + [
            pltpu.VMEM((HK, LB, BLK, 1024), bf16),
            pltpu.VMEM((HK, LB, BLK, 1024), bf16),
            pltpu.VMEM((8, LB * BLK, 1024), bf16),
            pltpu.VMEM((4, 256, GROUP * BLK), f32),
            pltpu.VMEM((LB, SEL + 1, BLK, HD), f32),
            pltpu.VMEM((3, BLK, HD), f32),
            pltpu.VMEM((LB, BLK, HD), f32),
            pltpu.VMEM((HK, 8, 32, HD), f32),
            pltpu.SMEM((LB, NB), jnp.int32),
        ]
        + [
            dma((4, HK)),
            dma((HK, 8)),
            dma((HK, 8)),
            dma((8,)),
            dma((8,)),
            dma((HK, 8)),
            dma((HK, 8)),
            dma((HK, 8)),
            dma((HK, 8)),
            dma((HK, 4)),
            dma((HK, 4)),
            dma((HK, 8)),
            dma((HK, 8)),
        ]
    )
    return pl.pallas_call(
        kernel,
        out_shape=jax.ShapeDtypeStruct((32, HK * HD), f32),
        in_specs=[any_ref, any_ref, any_ref, any_ref, smem, smem],
        out_specs=pl.BlockSpec(memory_space=pltpu.VMEM),
        scratch_shapes=scratch,
        compiler_params=pltpu.CompilerParams(
            collective_id=0, has_side_effects=True, vmem_limit_bytes=56 * 1024 * 1024
        ),
        cost_estimate=pl.CostEstimate(
            flops=6_500_000_000, bytes_accessed=9_000_000, transcendentals=8_400_000
        ),
    )(
        inputs,
        queries.reshape(LB, BLK, 4096),
        key_rows.reshape(LB, BLK, 512),
        out_grad.reshape(LB, BLK, 4096),
        sel_blocks,
        block_mask,
    )


def solution(mesh):
    placed = P(("outer", "inner"), None)
    return jax.shard_map(
        body, mesh=mesh, in_specs=(placed,) * 6, out_specs=P(("inner", "outer"), None), check_vma=False
    )
```

```python
import math

import jax
import jax.numpy as jnp
from jax import lax
from jax.experimental import pallas as pl
from jax.experimental.pallas import tpu as pltpu
from jax.sharding import PartitionSpec as P

HD = 128
GROUP = 8
HK = 4
BLK = 64
SEL = 16
NB = 32
LB = 4
SCALE = math.log2(math.e) / math.sqrt(HD)
MESH = pl.DeviceIdType.MESH
MID = jnp.bfloat16


def kernel(inputs, queries, key_rows, out_grad, sel, mask, out_ref, *scratch):
    scratch = list(scratch)

    def take(count):
        taken = scratch[:count]
        del scratch[:count]
        return taken

    keys = take(HK)
    give = take(HK)
    came = take(HK)
    value = take(HK)
    part = take(HK)
    part_in = take(HK)
    mid = take(HK)
    mid_in = take(HK)
    low = take(HK)
    low_in = take(HK)
    (q_ref, g_ref, xa_ref, xb_ref, st_ref, contrib, bias, vacc, inverse) = take(9)
    (loc, key_s, key_r, xa_s, xa_r, xb_s, xb_r, give_s, give_r, val_s, val_r) = take(11)
    (p1_s, p1_r, p2_s, p2_r, p3_s, p3_r) = take(6)

    outer, inner = lax.axis_index("outer"), lax.axis_index("inner")
    core, xlo, z = lax.rem(outer, 2), lax.rem(outer // 2, 2), outer // 4
    y, xhi = inner // 2, lax.rem(inner, 2)
    x, zl, zh = xhi * 2 + xlo, lax.rem(z, 2), z // 2
    member = zl * 2 + core

    def device(z_, xlo_, core_, y_, xhi_):
        return (z_ * 4 + xlo_ * 2 + core_, y_ * 2 + xhi_)

    def across(x_):
        return device(z, lax.rem(x_, 2), core, y, x_ // 2)

    def mate(dz, dc):
        return (1 - zl if dz else zl), (1 - core if dc else core)

    def remote(src, dst, send, recv, target):
        return pltpu.make_async_remote_copy(
            src_ref=src, dst_ref=dst, send_sem=send, recv_sem=recv, device_id=target, device_id_type=MESH
        )

    barrier = pltpu.get_barrier_semaphore()

    def greet(target):
        pl.semaphore_signal(barrier, inc=1, device_id=target, device_id_type=MESH)

    for dz in (4, 3, 5, 2, 6):
        for dc in range(2):
            greet(device(lax.rem(z + dz, 8), xlo, (1 - core if dc else core), y, xhi))
    for d in range(1, 8):
        greet((outer, lax.rem(inner + d, 8)))
    for dz, dc in ((1, 0), (1, 1), (7, 0), (7, 1), (0, 1)):
        greet(device(lax.rem(z + dz, 8), xlo, (1 - core if dc else core), y, xhi))
    for dx in (1, 3):
        greet(across(lax.rem(x + dx, 4)))

    q_loads = [
        pltpu.make_async_copy(
            queries.at[:, :, pl.ds(g * 1024, 1024)], q_ref.at[g], loc.at[0, g]
        )
        for g in range(HK)
    ]
    g_loads = [
        pltpu.make_async_copy(
            out_grad.at[:, :, pl.ds(g * 1024, 1024)], g_ref.at[g], loc.at[1, g]
        )
        for g in range(HK)
    ]
    k_loads = [
        pltpu.make_async_copy(
            key_rows.at[:, :, pl.ds(g * HD, HD)], keys[g].at[pl.ds(inner * LB, LB)], loc.at[2, g]
        )
        for g in range(HK)
    ]
    def columns_a(blk, m):
        return inputs.at[:, pl.ds(pl.multiple_of(blk * 1024 + (m // 2) * 512 + (m % 2) * 128, 128), 128)]

    def columns_b(blk, c):
        return inputs.at[:, pl.ds(pl.multiple_of(blk * 1024 + 256 + c * 512, 256), 256)]

    x_loads = []
    for blk in range(8):
        x_loads += [
            pltpu.make_async_copy(columns_a(blk, member), xa_ref.at[blk, member], loc.at[3, blk]),
            pltpu.make_async_copy(columns_b(blk, core), xb_ref.at[blk, core], loc.at[4, blk]),
        ]
    for g in range(HK):
        k_loads[g].start()
        q_loads[g].start()
        g_loads[g].start()

    pl.semaphore_wait(barrier, 24)

    def key_copy(g, d):
        return remote(
            key_rows.at[:, :, pl.ds(g * HD, HD)],
            keys[g].at[pl.ds(inner * LB, LB)],
            key_s.at[g, d],
            key_r.at[g, d],
            (outer, lax.rem(inner + d, 8)),
        )

    def key_arrival(g, d):
        src = lax.rem(inner + 8 - d, 8)
        return remote(
            key_rows.at[:, :, pl.ds(g * HD, HD)],
            keys[g].at[pl.ds(src * LB, LB)],
            key_s.at[g, d],
            key_r.at[g, d],
            (outer, src),
        )

    def key_goes(d):
        return inner + d < 8

    def key_comes(d):
        return inner - d >= 0

    def send_keys(g):
        for d in range(1, 8):

            @pl.when(key_goes(d))
            def _():
                key_copy(g, d).start()

    send_keys(0)

    mates = [(0, 1), (1, 0), (1, 1)]

    def xa_copy(blk, dz, dc):
        pz, pc = mate(dz, dc)
        return remote(
            columns_a(blk, pz * 2 + pc),
            xa_ref.at[blk, member],
            xa_s.at[dz * 2 + dc, blk],
            xa_r.at[dz * 2 + dc, blk],
            device(zh * 2 + pz, xlo, pc, y, xhi),
        )

    def xa_arrival(blk, dz, dc):
        sz, sc = mate(dz, dc)
        return remote(
            columns_a(blk, member),
            xa_ref.at[blk, sz * 2 + sc],
            xa_s.at[dz * 2 + dc, blk],
            xa_r.at[dz * 2 + dc, blk],
            device(zh * 2 + sz, xlo, sc, y, xhi),
        )

    def xb_copy(blk):
        return remote(
            columns_b(blk, 1 - core),
            xb_ref.at[blk, core],
            xb_s.at[blk],
            xb_r.at[blk],
            device(z, xlo, 1 - core, y, xhi),
        )

    def xb_arrival(blk):
        return remote(
            columns_b(blk, core),
            xb_ref.at[blk, 1 - core],
            xb_s.at[blk],
            xb_r.at[blk],
            device(z, xlo, 1 - core, y, xhi),
        )

    for dz, dc in mates[::-1]:
        for blk in range(8):
            xa_copy(blk, dz, dc).start()
    for blk in range(8):
        xb_copy(blk).start()
    for load in x_loads:
        load.start()

    for qb in range(LB):
        named = [jnp.where(mask[qb, s] == 1, sel[qb, s], -1) for s in range(SEL)]

        def invert(kb, carry):
            found = jnp.int32(SEL)
            for s in range(SEL):
                found = jnp.where(named[s] == kb, jnp.int32(s), found)
            inverse[qb, kb] = found
            return carry

        lax.fori_loop(0, inner * LB + LB, invert, 0)
    key_at = lax.broadcasted_iota(jnp.int32, (BLK, HD), 0)
    query_at = lax.rem(lax.broadcasted_iota(jnp.int32, (BLK, HD), 1), BLK)
    bias[0] = jnp.zeros((BLK, HD), jnp.float32)
    bias[1] = jnp.where(key_at <= query_at, 0.0, -1e30).astype(jnp.float32)
    bias[2] = jnp.full((BLK, HD), -1e30, jnp.float32)
    for qb in range(LB):
        contrib[qb, SEL] = jnp.zeros((BLK, HD), jnp.float32)

    def heads(ref, g, qb):
        return jnp.concatenate([ref[g, qb, :, pl.ds(h * HD, HD)] for h in range(GROUP)], axis=0)

    def attend(g):
        def one(qb, carry):
            place = inner * LB + qb
            query = heads(q_ref, g, qb)
            top = jnp.full((8, GROUP * BLK), -3e38, jnp.float32)
            for quad in range(4):
                picked, masks = [], []
                for s in range(4 * quad, 4 * quad + 4):
                    used = mask[qb, s] == 1
                    block = sel[qb, s]
                    picked.append(keys[g][jnp.where(used, block, place)])
                    kind = jnp.where(used, jnp.where(block == place, 1, 0), 2)
                    masks.append(bias[kind])
                scores = lax.dot_general(
                    jnp.concatenate(picked, axis=0),
                    query,
                    (((1,), (1,)), ((), ())),
                    preferred_element_type=jnp.float32,
                )
                shift = jnp.concatenate(masks, axis=0)
                scores = scores + jnp.concatenate([shift] * 4, axis=1)
                st_ref[quad] = scores
                top = jnp.maximum(top, jnp.max(scores.reshape(32, 8, GROUP * BLK), axis=0))
            top = jnp.max(top, axis=0, keepdims=True)
            total = jnp.zeros((8, GROUP * BLK), jnp.float32)
            for quad in range(4):
                weights = jnp.exp2((st_ref[quad] - top) * SCALE)
                st_ref[quad] = weights
                total = total + jnp.sum(weights.reshape(32, 8, GROUP * BLK), axis=0)
            norm = 1.0 / jnp.sum(total, axis=0, keepdims=True)
            grad = heads(g_ref, g, qb)
            for quad in range(4):
                probs = (st_ref[quad] * norm).astype(jnp.bfloat16)
                done = jnp.dot(probs, grad, preferred_element_type=jnp.float32)
                contrib[qb, pl.ds(4 * quad, 4)] = done.reshape(4, BLK, HD)
            return carry

        lax.fori_loop(0, LB, one, 0)

    def give_copy(g, j):
        d = inner - j
        return remote(
            give[g].at[j], came[g].at[d - 1], give_s.at[g, d], give_r.at[g, d], (outer, j)
        )

    def give_arrival(g, d):
        src = lax.rem(inner + d, 8)
        return remote(
            give[g].at[src], came[g].at[d - 1], give_s.at[g, d], give_r.at[g, d], (outer, src)
        )

    def terms_of(kb):
        terms = [contrib[qb, inverse[qb, kb]] for qb in range(LB)]
        return (terms[0] + terms[1]) + (terms[2] + terms[3])

    def hand_out(g):
        def owner(j, carry):
            for t in range(LB):
                give[g][j, t] = terms_of(j * LB + t).astype(jnp.bfloat16)
            give_copy(g, j).start()
            return carry

        lax.fori_loop(0, inner, owner, 0)
        for t in range(LB):
            vacc[g, t] = terms_of(inner * LB + t)

    def value_copy(g, dz, dc):
        pz, pc = mate(dz, dc)
        return remote(
            value[g].at[member],
            value[g].at[member],
            val_s.at[g, dz * 2 + dc],
            val_r.at[g, dz * 2 + dc],
            device(zh * 2 + pz, xlo, pc, y, xhi),
        )

    def value_arrival(g, dz, dc):
        sz, sc = mate(dz, dc)
        return remote(
            value[g].at[sz * 2 + sc],
            value[g].at[sz * 2 + sc],
            val_s.at[g, dz * 2 + dc],
            val_r.at[g, dz * 2 + dc],
            device(zh * 2 + sz, xlo, sc, y, xhi),
        )

    def own(g):
        for d in range(1, 8):

            @pl.when(inner + d < 8)
            def _():
                give_arrival(g, d).wait_recv()
                vacc[g] += came[g][d - 1].astype(jnp.float32)

        value[g][member] = vacc[g].reshape(LB * BLK, HD).astype(jnp.bfloat16)
        for dz, dc in mates:
            value_copy(g, dz, dc).start()

    place_of = (y, x)

    def along(u, at_):
        return (outer, at_ * 2 + xhi) if u == 0 else across(at_)

    def part_copy(g, u, to):
        return remote(
            part[g].at[u, to],
            part_in[g].at[u, place_of[u]],
            p1_s.at[g, u * 4 + to],
            p1_r.at[g, u * 4 + place_of[u]],
            along(u, to),
        )

    def part_arrival(g, u, src):
        return remote(
            part[g].at[u, src],
            part_in[g].at[u, src],
            p1_s.at[g, u * 4 + src],
            p1_r.at[g, u * 4 + src],
            along(u, src),
        )

    def inputs_here():
        for load in x_loads:
            load.wait()
        for blk in range(8):
            xb_arrival(blk).wait_recv()
            for dz, dc in mates:
                xa_arrival(blk, dz, dc).wait_recv()

    def term_of(low_, wide):
        term = lax.dot_general(
            low_, wide, (((0,), (0,)), ((), ())), preferred_element_type=jnp.float32
        )
        return term.T.astype(jnp.bfloat16)

    def multiply(g):
        for dz, dc in mates:
            value_arrival(g, dz, dc).wait_recv()
        four = value[g][...].reshape(4 * LB * BLK, HD)
        two = value[g][pl.ds(2 * zl, 2)].reshape(2 * LB * BLK, HD)
        for to in range(4):
            wide = jnp.concatenate([xa_ref[2 * to], xa_ref[2 * to + 1]], axis=-1)
            rows = term_of(four, wide.reshape(4 * LB * BLK, 256)).reshape(4, 2, 32, HD)
            part[g][0, to, :, 2] = rows[:, 0]
            for at_ in range(4):
                part[g][1, at_, to, 2] = rows[at_, 1]
            for hi in range(2):
                rows = term_of(two, xb_ref[2 * to + hi].reshape(2 * LB * BLK, 256))
                rows = rows.reshape(2, 2, 2, 32, HD)
                for lo in range(2):
                    part[g][0, to, 2 * hi + lo, pl.ds(0, 2)] = rows[0, lo]
                    part[g][1, 2 * hi + lo, to, pl.ds(0, 2)] = rows[1, lo]
            send_part(g, 0, to)
        for to in range(4):
            send_part(g, 1, to)

    def send_part(g, u, to):
        @pl.when(place_of[u] != to)
        def _():
            part_copy(g, u, to).start()

        @pl.when(place_of[u] == to)
        def _():
            part_in[g][u, to] = part[g][u, to]

    def mid_copy(g, u, d):
        to = lax.rem(place_of[1 - u] + d, 4)
        return remote(
            mid[g].at[u, to],
            mid_in[g].at[u, d],
            p2_s.at[g, u * 4 + d],
            p2_r.at[g, u * 4 + d],
            along(1 - u, to),
        )

    def mid_arrival(g, u, d):
        src = lax.rem(place_of[1 - u] + 4 - d, 4)
        return remote(
            mid[g].at[u, src],
            mid_in[g].at[u, d],
            p2_s.at[g, u * 4 + d],
            p2_r.at[g, u * 4 + d],
            along(1 - u, src),
        )

    def sum_first(g):
        for u in range(2):
            for src in range(4):

                @pl.when(place_of[u] != src)
                def _():
                    part_arrival(g, u, src).wait_recv()

            terms = [part_in[g][u, k].astype(jnp.float32) for k in range(4)]
            total = (terms[0] + terms[1]) + (terms[2] + terms[3])
            mid[g][u] = total.astype(MID)
            for d in range(1, 4):
                mid_copy(g, u, d).start()

    def low_target(u, k):
        return (4 * zl + core, u) if k == 2 else (4 * core + 2 + u, k)

    def low_copy(g, u, k):
        to_z, to_core = low_target(u, k)
        return remote(
            low[g].at[u, k],
            low_in[g].at[z],
            p3_s.at[g, u * 3 + k],
            p3_r.at[g, z],
            device(to_z, xlo, to_core, y, xhi),
        )

    def low_stays(u, k):
        to_z, to_core = low_target(u, k)
        return (to_z == z) & (to_core == core)

    wide_z = lax.rem(z, 4) >= 2
    from_core = jnp.where(wide_z, z // 4, lax.rem(z, 2))

    def low_comes(src):
        return wide_z | (src % 2 == z // 4)

    def low_is_own(src):
        return (src == z) & (from_core == core)

    def low_arrival(g, src):
        return remote(
            low[g].at[0, 0],
            low_in[g].at[src],
            p3_s.at[g, 0],
            p3_r.at[g, src],
            device(src, xlo, from_core, y, xhi),
        )

    def sum_second(g):
        for u in range(2):
            total = mid[g][u, place_of[1 - u]].astype(jnp.float32)
            for d in range(1, 4):
                mid_arrival(g, u, d).wait_recv()
                total = total + mid_in[g][u, d].astype(jnp.float32)
            low[g][u] = total
            for k in range(3):

                @pl.when(jnp.logical_not(low_stays(u, k)))
                def _():
                    low_copy(g, u, k).start()

                @pl.when(low_stays(u, k))
                def _():
                    low_in[g][z] = low[g][u, k]

    def sum_z(g):
        column = pl.ds(g * HD, HD)
        out_ref[:, column] = jnp.zeros((32, HD), jnp.float32)
        for src in range(8):

            @pl.when(low_comes(src) & jnp.logical_not(low_is_own(src)))
            def _():
                low_arrival(g, src).wait_recv()

            @pl.when(low_comes(src))
            def _():
                out_ref[:, column] += low_in[g][src]

    def start_of(g):
        for d in range(1, 8):

            @pl.when(key_comes(d))
            def _():
                key_arrival(g, d).wait_recv()

        k_loads[g].wait()
        q_loads[g].wait()
        g_loads[g].wait()

    def next_keys(g):
        for d in range(1, 8):

            @pl.when(key_goes(d))
            def _():
                key_copy(g - 1, d).wait_send()
                key_copy(g, d).start()

    def step(g):
        start_of(g)
        attend(g)
        hand_out(g)
        if g + 2 < HK:
            next_keys(g + 2)

    next_keys(1)
    step(0)
    step(1)
    own(0)
    step(2)
    own(1)
    inputs_here()
    multiply(0)
    step(3)
    own(2)
    multiply(1)
    sum_first(0)
    own(3)
    multiply(2)
    sum_first(1)
    multiply(3)
    sum_second(0)
    sum_first(2)
    sum_second(1)
    sum_first(3)
    sum_second(2)
    sum_second(3)
    for g in range(HK):
        sum_z(g)

    for g in range(HK):
        for d in range(1, 8):

            if g + 1 == HK:

                @pl.when(key_goes(d))
                def _():
                    key_copy(g, d).wait_send()

            @pl.when(inner - d >= 0)
            def _():
                give_copy(g, inner - d).wait_send()

        for dz, dc in mates:
            value_copy(g, dz, dc).wait_send()
        for u in range(2):
            for to in range(4):

                @pl.when(place_of[u] != to)
                def _():
                    part_copy(g, u, to).wait_send()

            for d in range(1, 4):
                mid_copy(g, u, d).wait_send()
            for k in range(3):

                @pl.when(jnp.logical_not(low_stays(u, k)))
                def _():
                    low_copy(g, u, k).wait_send()

    for blk in range(8):
        xb_copy(blk).wait_send()
        for dz, dc in mates:
            xa_copy(blk, dz, dc).wait_send()


def body(inputs, queries, key_rows, out_grad, sel_blocks, block_mask):
    any_ref = pl.BlockSpec(memory_space=pl.ANY)
    smem = pl.BlockSpec(memory_space=pltpu.SMEM)
    bf16, f32 = jnp.bfloat16, jnp.float32
    dma = pltpu.SemaphoreType.DMA
    scratch = (
        [pltpu.VMEM((NB, BLK, HD), bf16)] * HK
        + [pltpu.VMEM((8, LB, BLK, HD), bf16)] * HK
        + [pltpu.VMEM((7, LB, BLK, HD), bf16)] * HK
        + [pltpu.VMEM((4, LB * BLK, HD), bf16)] * HK
        + [pltpu.VMEM((2, 4, 4, 3, 32, HD), bf16)] * HK
        + [pltpu.VMEM((2, 4, 4, 3, 32, HD), bf16)] * HK
        + [pltpu.VMEM((2, 4, 3, 32, HD), MID)] * HK
        + [pltpu.VMEM((2, 4, 3, 32, HD), MID)] * HK
        + [pltpu.VMEM((2, 3, 32, HD), f32)] * HK
        + [pltpu.VMEM((8, 32, HD), f32)] * HK
        + [
            pltpu.VMEM((HK, LB, BLK, 1024), bf16),
            pltpu.VMEM((HK, LB, BLK, 1024), bf16),
            pltpu.VMEM((8, 4, LB * BLK, 128), bf16),
            pltpu.VMEM((8, 2, LB * BLK, 256), bf16),
            pltpu.VMEM((4, 256, GROUP * BLK), f32),
            pltpu.VMEM((LB, SEL + 1, BLK, HD), f32),
            pltpu.VMEM((3, BLK, HD), f32),
            pltpu.VMEM((HK, LB, BLK, HD), f32),
            pltpu.SMEM((LB, NB), jnp.int32),
        ]
        + [
            dma((5, 8)),
            dma((HK, 8)),
            dma((HK, 8)),
            dma((4, 8)),
            dma((4, 8)),
            dma((8,)),
            dma((8,)),
            dma((HK, 8)),
            dma((HK, 8)),
            dma((HK, 4)),
            dma((HK, 4)),
        ]
        + [dma((HK, 8))] * 6
    )
    return pl.pallas_call(
        kernel,
        out_shape=jax.ShapeDtypeStruct((32, HK * HD), f32),
        in_specs=[any_ref, any_ref, any_ref, any_ref, smem, smem],
        out_specs=pl.BlockSpec(memory_space=pltpu.VMEM),
        scratch_shapes=scratch,
        compiler_params=pltpu.CompilerParams(
            collective_id=0, has_side_effects=True, vmem_limit_bytes=56 * 1024 * 1024
        ),
        cost_estimate=pl.CostEstimate(
            flops=6_500_000_000, bytes_accessed=9_000_000, transcendentals=8_400_000
        ),
    )(
        inputs,
        queries.reshape(LB, BLK, 4096),
        key_rows.reshape(LB, BLK, 512),
        out_grad.reshape(LB, BLK, 4096),
        sel_blocks,
        block_mask,
    )


def solution(mesh):
    placed = P(("outer", "inner"), None)
    return jax.shard_map(
        body, mesh=mesh, in_specs=(placed,) * 6, out_specs=P(("inner", "outer"), None), check_vma=False
    )
```

```python
import math

import jax
import jax.numpy as jnp
from jax import lax
from jax.experimental import pallas as pl
from jax.experimental.pallas import tpu as pltpu
from jax.sharding import PartitionSpec as P

HD = 128
GROUP = 8
HK = 4
BLK = 64
SEL = 16
NB = 32
LB = 4
SCALE = math.log2(math.e) / math.sqrt(HD)
MESH = pl.DeviceIdType.MESH
MID = jnp.bfloat16


def kernel(inputs, queries, key_rows, out_grad, sel_in, mask_in, out_ref, *scratch):
    scratch = list(scratch)

    def take(count):
        taken = scratch[:count]
        del scratch[:count]
        return taken

    keys = take(HK)
    give = take(HK)
    came = take(HK)
    value = take(HK)
    part = take(HK)
    part_in = take(HK)
    mid = take(HK)
    mid_in = take(HK)
    low = take(HK)
    low_in = take(HK)
    (q_ref, g_ref, xa_ref, xb_ref, st_ref, contrib, bias, vacc, inverse, sel, mask) = take(11)
    (loc, key_s, key_r, xa_s, xa_r, xb_s, xb_r, give_s, give_r, val_s, val_r) = take(11)
    (p1_s, p1_r, p2_s, p2_r, p3_s, p3_r) = take(6)

    outer, inner = lax.axis_index("outer"), lax.axis_index("inner")
    core, xlo, z = lax.rem(outer, 2), lax.rem(outer // 2, 2), outer // 4
    y, xhi = inner // 2, lax.rem(inner, 2)
    x, zl, zh = xhi * 2 + xlo, lax.rem(z, 2), z // 2
    member = zl * 2 + core

    def device(z_, xlo_, core_, y_, xhi_):
        return (z_ * 4 + xlo_ * 2 + core_, y_ * 2 + xhi_)

    def across(x_):
        return device(z, lax.rem(x_, 2), core, y, x_ // 2)

    def mate(dz, dc):
        return (1 - zl if dz else zl), (1 - core if dc else core)

    def remote(src, dst, send, recv, target):
        return pltpu.make_async_remote_copy(
            src_ref=src, dst_ref=dst, send_sem=send, recv_sem=recv, device_id=target, device_id_type=MESH
        )

    barrier = pltpu.get_barrier_semaphore()

    def greet(target):
        pl.semaphore_signal(barrier, inc=1, device_id=target, device_id_type=MESH)

    for dz in (4, 3, 5, 2, 6):
        for dc in range(2):
            greet(device(lax.rem(z + dz, 8), xlo, (1 - core if dc else core), y, xhi))
    for d in range(1, 8):
        greet((outer, lax.rem(inner + d, 8)))
    for dz, dc in ((1, 0), (1, 1), (7, 0), (7, 1), (0, 1)):
        greet(device(lax.rem(z + dz, 8), xlo, (1 - core if dc else core), y, xhi))
    for dx in (1, 3):
        greet(across(lax.rem(x + dx, 4)))

    q_loads = [
        pltpu.make_async_copy(
            queries.at[:, :, pl.ds(g * 1024, 1024)], q_ref.at[g], loc.at[0, g]
        )
        for g in range(HK)
    ]
    g_loads = [
        pltpu.make_async_copy(
            out_grad.at[:, :, pl.ds(g * 1024, 1024)], g_ref.at[g], loc.at[1, g]
        )
        for g in range(HK)
    ]
    k_loads = [
        pltpu.make_async_copy(
            key_rows.at[:, :, pl.ds(g * HD, HD)], keys[g].at[pl.ds(inner * LB, LB)], loc.at[2, g]
        )
        for g in range(HK)
    ]
    def columns_a(blk, m):
        return inputs.at[:, pl.ds(pl.multiple_of(blk * 1024 + (m // 2) * 512 + (m % 2) * 128, 128), 128)]

    def columns_b(blk, c):
        return inputs.at[:, pl.ds(pl.multiple_of(blk * 1024 + 256 + c * 512, 256), 256)]

    x_loads = []
    for blk in range(8):
        x_loads += [
            pltpu.make_async_copy(columns_a(blk, member), xa_ref.at[blk, member], loc.at[3, blk]),
            pltpu.make_async_copy(columns_b(blk, core), xb_ref.at[blk, core], loc.at[4, blk]),
        ]
    choices = [
        pltpu.make_async_copy(sel_in, sel, loc.at[0, 4]),
        pltpu.make_async_copy(mask_in, mask, loc.at[0, 5]),
    ]
    for choice in choices:
        choice.start()
    for g in range(HK):
        k_loads[g].start()
        q_loads[g].start()
        g_loads[g].start()

    pl.semaphore_wait(barrier, 24)

    def key_copy(g, d):
        return remote(
            key_rows.at[:, :, pl.ds(g * HD, HD)],
            keys[g].at[pl.ds(inner * LB, LB)],
            key_s.at[g, d],
            key_r.at[g, d],
            (outer, lax.rem(inner + d, 8)),
        )

    def key_arrival(g, d):
        src = lax.rem(inner + 8 - d, 8)
        return remote(
            key_rows.at[:, :, pl.ds(g * HD, HD)],
            keys[g].at[pl.ds(src * LB, LB)],
            key_s.at[g, d],
            key_r.at[g, d],
            (outer, src),
        )

    def key_goes(d):
        return inner + d < 8

    def key_comes(d):
        return inner - d >= 0

    def send_keys(g):
        for d in range(1, 8):

            @pl.when(key_goes(d))
            def _():
                key_copy(g, d).start()

    send_keys(0)

    mates = [(0, 1), (1, 0), (1, 1)]

    def xa_copy(blk, dz, dc):
        pz, pc = mate(dz, dc)
        return remote(
            columns_a(blk, pz * 2 + pc),
            xa_ref.at[blk, member],
            xa_s.at[dz * 2 + dc, blk],
            xa_r.at[dz * 2 + dc, blk],
            device(zh * 2 + pz, xlo, pc, y, xhi),
        )

    def xa_arrival(blk, dz, dc):
        sz, sc = mate(dz, dc)
        return remote(
            columns_a(blk, member),
            xa_ref.at[blk, sz * 2 + sc],
            xa_s.at[dz * 2 + dc, blk],
            xa_r.at[dz * 2 + dc, blk],
            device(zh * 2 + sz, xlo, sc, y, xhi),
        )

    def xb_copy(blk):
        return remote(
            columns_b(blk, 1 - core),
            xb_ref.at[blk, core],
            xb_s.at[blk],
            xb_r.at[blk],
            device(z, xlo, 1 - core, y, xhi),
        )

    def xb_arrival(blk):
        return remote(
            columns_b(blk, core),
            xb_ref.at[blk, 1 - core],
            xb_s.at[blk],
            xb_r.at[blk],
            device(z, xlo, 1 - core, y, xhi),
        )

    for dz, dc in mates[::-1]:
        for blk in range(8):
            xa_copy(blk, dz, dc).start()
    for blk in range(8):
        xb_copy(blk).start()
    for load in x_loads:
        load.start()

    for choice in choices:
        choice.wait()

    for qb in range(LB):
        named = [jnp.where(mask[qb, s] == 1, sel[qb, s], -1) for s in range(SEL)]

        def invert(kb, carry):
            found = jnp.int32(SEL)
            for s in range(SEL):
                found = jnp.where(named[s] == kb, jnp.int32(s), found)
            inverse[qb, kb] = found
            return carry

        lax.fori_loop(0, inner * LB + LB, invert, 0)
    key_at = lax.broadcasted_iota(jnp.int32, (BLK, HD), 0)
    query_at = lax.rem(lax.broadcasted_iota(jnp.int32, (BLK, HD), 1), BLK)
    bias[0] = jnp.zeros((BLK, HD), jnp.float32)
    bias[1] = jnp.where(key_at <= query_at, 0.0, -1e30).astype(jnp.float32)
    bias[2] = jnp.full((BLK, HD), -1e30, jnp.float32)
    for qb in range(LB):
        contrib[qb, SEL] = jnp.zeros((BLK, HD), jnp.float32)

    def heads(ref, g, qb):
        return jnp.concatenate([ref[g, qb, :, pl.ds(h * HD, HD)] for h in range(GROUP)], axis=0)

    def attend(g):
        def one(qb, carry):
            place = inner * LB + qb
            query = heads(q_ref, g, qb)
            top = jnp.full((8, GROUP * BLK), -3e38, jnp.float32)
            for quad in range(4):
                picked, masks = [], []
                for s in range(4 * quad, 4 * quad + 4):
                    used = mask[qb, s] == 1
                    block = sel[qb, s]
                    picked.append(keys[g][jnp.where(used, block, place)])
                    kind = jnp.where(used, jnp.where(block == place, 1, 0), 2)
                    masks.append(bias[kind])
                scores = lax.dot_general(
                    jnp.concatenate(picked, axis=0),
                    query,
                    (((1,), (1,)), ((), ())),
                    preferred_element_type=jnp.float32,
                )
                shift = jnp.concatenate(masks, axis=0)
                scores = scores + jnp.concatenate([shift] * 4, axis=1)
                st_ref[quad] = scores
                top = jnp.maximum(top, jnp.max(scores.reshape(32, 8, GROUP * BLK), axis=0))
            top = jnp.max(top, axis=0, keepdims=True)
            total = jnp.zeros((8, GROUP * BLK), jnp.float32)
            for quad in range(4):
                weights = jnp.exp2((st_ref[quad] - top) * SCALE)
                st_ref[quad] = weights
                total = total + jnp.sum(weights.reshape(32, 8, GROUP * BLK), axis=0)
            norm = 1.0 / jnp.sum(total, axis=0, keepdims=True)
            grad = heads(g_ref, g, qb)
            for quad in range(4):
                probs = (st_ref[quad] * norm).astype(jnp.bfloat16)
                done = jnp.dot(probs, grad, preferred_element_type=jnp.float32)
                contrib[qb, pl.ds(4 * quad, 4)] = done.reshape(4, BLK, HD)
            return carry

        lax.fori_loop(0, LB, one, 0)

    def give_copy(g, j):
        d = inner - j
        return remote(
            give[g].at[j], came[g].at[d - 1], give_s.at[g, d], give_r.at[g, d], (outer, j)
        )

    def give_arrival(g, d):
        src = lax.rem(inner + d, 8)
        return remote(
            give[g].at[src], came[g].at[d - 1], give_s.at[g, d], give_r.at[g, d], (outer, src)
        )

    def terms_of(kb):
        terms = [contrib[qb, inverse[qb, kb]] for qb in range(LB)]
        return (terms[0] + terms[1]) + (terms[2] + terms[3])

    def hand_out(g):
        def owner(j, carry):
            for t in range(LB):
                give[g][j, t] = terms_of(j * LB + t).astype(jnp.bfloat16)
            give_copy(g, j).start()
            return carry

        lax.fori_loop(0, inner, owner, 0)
        for t in range(LB):
            vacc[g, t] = terms_of(inner * LB + t)

    def value_copy(g, dz, dc):
        pz, pc = mate(dz, dc)
        return remote(
            value[g].at[member],
            value[g].at[member],
            val_s.at[g, dz * 2 + dc],
            val_r.at[g, dz * 2 + dc],
            device(zh * 2 + pz, xlo, pc, y, xhi),
        )

    def value_arrival(g, dz, dc):
        sz, sc = mate(dz, dc)
        return remote(
            value[g].at[sz * 2 + sc],
            value[g].at[sz * 2 + sc],
            val_s.at[g, dz * 2 + dc],
            val_r.at[g, dz * 2 + dc],
            device(zh * 2 + sz, xlo, sc, y, xhi),
        )

    def own(g):
        for d in range(1, 8):

            @pl.when(inner + d < 8)
            def _():
                give_arrival(g, d).wait_recv()
                vacc[g] += came[g][d - 1].astype(jnp.float32)

        value[g][member] = vacc[g].reshape(LB * BLK, HD).astype(jnp.bfloat16)
        for dz, dc in mates:
            value_copy(g, dz, dc).start()

    place_of = (y, x)

    def along(u, at_):
        return (outer, at_ * 2 + xhi) if u == 0 else across(at_)

    def part_copy(g, u, to):
        return remote(
            part[g].at[u, to],
            part_in[g].at[u, place_of[u]],
            p1_s.at[g, u * 4 + to],
            p1_r.at[g, u * 4 + place_of[u]],
            along(u, to),
        )

    def part_arrival(g, u, src):
        return remote(
            part[g].at[u, src],
            part_in[g].at[u, src],
            p1_s.at[g, u * 4 + src],
            p1_r.at[g, u * 4 + src],
            along(u, src),
        )

    def inputs_here():
        for load in x_loads:
            load.wait()
        for blk in range(8):
            xb_arrival(blk).wait_recv()
            for dz, dc in mates:
                xa_arrival(blk, dz, dc).wait_recv()

    def term_of(low_, wide):
        term = lax.dot_general(
            low_, wide, (((0,), (0,)), ((), ())), preferred_element_type=jnp.float32
        )
        return term.T.astype(jnp.bfloat16)

    def multiply(g):
        for dz, dc in mates:
            value_arrival(g, dz, dc).wait_recv()
        four = value[g][...].reshape(4 * LB * BLK, HD)
        two = value[g][pl.ds(2 * zl, 2)].reshape(2 * LB * BLK, HD)
        for to in range(4):
            wide = jnp.concatenate([xa_ref[2 * to], xa_ref[2 * to + 1]], axis=-1)
            rows = term_of(four, wide.reshape(4 * LB * BLK, 256)).reshape(4, 2, 32, HD)
            part[g][0, to, :, 2] = rows[:, 0]
            for at_ in range(4):
                part[g][1, at_, to, 2] = rows[at_, 1]
            for hi in range(2):
                rows = term_of(two, xb_ref[2 * to + hi].reshape(2 * LB * BLK, 256))
                rows = rows.reshape(2, 2, 2, 32, HD)
                for lo in range(2):
                    part[g][0, to, 2 * hi + lo, pl.ds(0, 2)] = rows[0, lo]
                    part[g][1, 2 * hi + lo, to, pl.ds(0, 2)] = rows[1, lo]
            send_part(g, 0, to)
        for to in range(4):
            send_part(g, 1, to)

    def send_part(g, u, to):
        @pl.when(place_of[u] != to)
        def _():
            part_copy(g, u, to).start()

        @pl.when(place_of[u] == to)
        def _():
            part_in[g][u, to] = part[g][u, to]

    def mid_copy(g, u, d):
        to = lax.rem(place_of[1 - u] + d, 4)
        return remote(
            mid[g].at[u, to],
            mid_in[g].at[u, d],
            p2_s.at[g, u * 4 + d],
            p2_r.at[g, u * 4 + d],
            along(1 - u, to),
        )

    def mid_arrival(g, u, d):
        src = lax.rem(place_of[1 - u] + 4 - d, 4)
        return remote(
            mid[g].at[u, src],
            mid_in[g].at[u, d],
            p2_s.at[g, u * 4 + d],
            p2_r.at[g, u * 4 + d],
            along(1 - u, src),
        )

    def sum_first(g):
        for u in range(2):
            for src in range(4):

                @pl.when(place_of[u] != src)
                def _():
                    part_arrival(g, u, src).wait_recv()

            terms = [part_in[g][u, k].astype(jnp.float32) for k in range(4)]
            total = (terms[0] + terms[1]) + (terms[2] + terms[3])
            mid[g][u] = total.astype(MID)
            for d in range(1, 4):
                mid_copy(g, u, d).start()

    def low_target(u, k):
        return (4 * zl + core, u) if k == 2 else (4 * core + 2 + u, k)

    def low_copy(g, u, k):
        to_z, to_core = low_target(u, k)
        return remote(
            low[g].at[u, k],
            low_in[g].at[z],
            p3_s.at[g, u * 3 + k],
            p3_r.at[g, z],
            device(to_z, xlo, to_core, y, xhi),
        )

    def low_stays(u, k):
        to_z, to_core = low_target(u, k)
        return (to_z == z) & (to_core == core)

    wide_z = lax.rem(z, 4) >= 2
    from_core = jnp.where(wide_z, z // 4, lax.rem(z, 2))

    def low_comes(src):
        return wide_z | (src % 2 == z // 4)

    def low_is_own(src):
        return (src == z) & (from_core == core)

    def low_arrival(g, src):
        return remote(
            low[g].at[0, 0],
            low_in[g].at[src],
            p3_s.at[g, 0],
            p3_r.at[g, src],
            device(src, xlo, from_core, y, xhi),
        )

    def sum_second(g):
        for u in range(2):
            total = mid[g][u, place_of[1 - u]].astype(jnp.float32)
            for d in range(1, 4):
                mid_arrival(g, u, d).wait_recv()
                total = total + mid_in[g][u, d].astype(jnp.float32)
            low[g][u] = total.astype(MID)
            for k in range(3):

                @pl.when(jnp.logical_not(low_stays(u, k)))
                def _():
                    low_copy(g, u, k).start()

                @pl.when(low_stays(u, k))
                def _():
                    low_in[g][z] = low[g][u, k]

    def sum_z(g):
        column = pl.ds(g * HD, HD)
        out_ref[:, column] = jnp.zeros((32, HD), jnp.float32)
        for src in range(8):

            @pl.when(low_comes(src) & jnp.logical_not(low_is_own(src)))
            def _():
                low_arrival(g, src).wait_recv()

            @pl.when(low_comes(src))
            def _():
                out_ref[:, column] += low_in[g][src].astype(jnp.float32)

    def start_of(g):
        for d in range(1, 8):

            @pl.when(key_comes(d))
            def _():
                key_arrival(g, d).wait_recv()

        k_loads[g].wait()
        q_loads[g].wait()
        g_loads[g].wait()

    def next_keys(g):
        for d in range(1, 8):

            @pl.when(key_goes(d))
            def _():
                key_copy(g - 1, d).wait_send()
                key_copy(g, d).start()

    def step(g):
        start_of(g)
        attend(g)
        hand_out(g)
        if g + 2 < HK:
            next_keys(g + 2)

    next_keys(1)
    def early_left(g):
        for d in range(1, 8):
            if g + 1 == HK:

                @pl.when(key_goes(d))
                def _():
                    key_copy(g, d).wait_send()

            @pl.when(inner - d >= 0)
            def _():
                give_copy(g, inner - d).wait_send()

        for dz, dc in mates:
            value_copy(g, dz, dc).wait_send()

    def inputs_left():
        for blk in range(8):
            xb_copy(blk).wait_send()
            for dz, dc in mates:
                xa_copy(blk, dz, dc).wait_send()

    def sums_left(g):
        for u in range(2):
            for to in range(4):

                @pl.when(place_of[u] != to)
                def _():
                    part_copy(g, u, to).wait_send()

            for d in range(1, 4):
                mid_copy(g, u, d).wait_send()

    def low_left(g):
        for u in range(2):
            for k in range(3):

                @pl.when(jnp.logical_not(low_stays(u, k)))
                def _():
                    low_copy(g, u, k).wait_send()

    step(0)
    step(1)
    own(0)
    step(2)
    own(1)
    step(3)
    inputs_here()
    multiply(0)
    multiply(1)
    own(2)
    sum_first(0)
    own(3)
    inputs_left()
    multiply(2)
    sum_first(1)
    sum_second(0)
    multiply(3)
    sum_first(2)
    sum_second(1)
    for g in range(HK):
        early_left(g)
    sum_first(3)
    sum_second(2)
    for g in range(3):
        sums_left(g)
    sum_z(0)
    sum_z(1)
    sum_second(3)
    sums_left(3)
    sum_z(2)
    for g in range(3):
        low_left(g)
    sum_z(3)
    low_left(3)


def body(inputs, queries, key_rows, out_grad, sel_blocks, block_mask):
    any_ref = pl.BlockSpec(memory_space=pl.ANY)
    bf16, f32 = jnp.bfloat16, jnp.float32
    dma = pltpu.SemaphoreType.DMA
    scratch = (
        [pltpu.VMEM((NB, BLK, HD), bf16)] * HK
        + [pltpu.VMEM((8, LB, BLK, HD), bf16)] * HK
        + [pltpu.VMEM((7, LB, BLK, HD), bf16)] * HK
        + [pltpu.VMEM((4, LB * BLK, HD), bf16)] * HK
        + [pltpu.VMEM((2, 4, 4, 3, 32, HD), bf16)] * HK
        + [pltpu.VMEM((2, 4, 4, 3, 32, HD), bf16)] * HK
        + [pltpu.VMEM((2, 4, 3, 32, HD), MID)] * HK
        + [pltpu.VMEM((2, 4, 3, 32, HD), MID)] * HK
        + [pltpu.VMEM((2, 3, 32, HD), MID)] * HK
        + [pltpu.VMEM((8, 32, HD), MID)] * HK
        + [
            pltpu.VMEM((HK, LB, BLK, 1024), bf16),
            pltpu.VMEM((HK, LB, BLK, 1024), bf16),
            pltpu.VMEM((8, 4, LB * BLK, 128), bf16),
            pltpu.VMEM((8, 2, LB * BLK, 256), bf16),
            pltpu.VMEM((4, 256, GROUP * BLK), f32),
            pltpu.VMEM((LB, SEL + 1, BLK, HD), f32),
            pltpu.VMEM((3, BLK, HD), f32),
            pltpu.VMEM((HK, LB, BLK, HD), f32),
            pltpu.SMEM((LB, NB), jnp.int32),
            pltpu.SMEM((LB, SEL), jnp.int32),
            pltpu.SMEM((LB, SEL), jnp.int32),
        ]
        + [
            dma((5, 8)),
            dma((HK, 8)),
            dma((HK, 8)),
            dma((4, 8)),
            dma((4, 8)),
            dma((8,)),
            dma((8,)),
            dma((HK, 8)),
            dma((HK, 8)),
            dma((HK, 4)),
            dma((HK, 4)),
        ]
        + [dma((HK, 8))] * 6
    )
    return pl.pallas_call(
        kernel,
        out_shape=jax.ShapeDtypeStruct((32, HK * HD), f32),
        in_specs=[any_ref] * 6,
        out_specs=pl.BlockSpec(memory_space=pltpu.VMEM),
        scratch_shapes=scratch,
        compiler_params=pltpu.CompilerParams(
            collective_id=0, has_side_effects=True, vmem_limit_bytes=56 * 1024 * 1024
        ),
        cost_estimate=pl.CostEstimate(
            flops=6_500_000_000, bytes_accessed=9_000_000, transcendentals=8_400_000
        ),
    )(
        inputs,
        queries.reshape(LB, BLK, 4096),
        key_rows.reshape(LB, BLK, 512),
        out_grad.reshape(LB, BLK, 4096),
        sel_blocks,
        block_mask,
    )


def solution(mesh):
    placed = P(("outer", "inner"), None)
    return jax.shard_map(
        body, mesh=mesh, in_specs=(placed,) * 6, out_specs=P(("inner", "outer"), None), check_vma=False
    )
```

```python
import math

import jax
import jax.numpy as jnp
from jax import lax
from jax.experimental import pallas as pl
from jax.experimental.pallas import tpu as pltpu
from jax.sharding import PartitionSpec as P

HD = 128
GROUP = 8
HK = 4
BLK = 64
SEL = 16
NB = 32
LB = 4
SCALE = math.log2(math.e) / math.sqrt(HD)
MESH = pl.DeviceIdType.MESH
MID = jnp.bfloat16


def kernel(inputs, queries, key_rows, out_grad, sel_in, mask_in, out_ref, *scratch):
    scratch = list(scratch)

    def take(count):
        taken = scratch[:count]
        del scratch[:count]
        return taken

    keys = take(HK)
    give = take(HK)
    came = take(HK)
    value = take(HK)
    part = take(HK)
    part_in = take(HK)
    mid = take(HK)
    mid_in = take(HK)
    low = take(HK)
    low_in = take(HK)
    (q_ref, g_ref, xa_ref, xb_ref, st_ref, contrib, bias, vacc, inverse, sel, mask) = take(11)
    (loc, key_s, key_r, xa_s, xa_r, xb_s, xb_r, give_s, give_r, val_s, val_r) = take(11)
    (p1_s, p1_r, p2_s, p2_r, p3_s, p3_r) = take(6)

    outer, inner = lax.axis_index("outer"), lax.axis_index("inner")
    core, xlo, z = lax.rem(outer, 2), lax.rem(outer // 2, 2), outer // 4
    y, xhi = inner // 2, lax.rem(inner, 2)
    x, zl, zh = xhi * 2 + xlo, lax.rem(z, 2), z // 2
    member = zl * 2 + core

    def device(z_, xlo_, core_, y_, xhi_):
        return (z_ * 4 + xlo_ * 2 + core_, y_ * 2 + xhi_)

    def across(x_):
        return device(z, lax.rem(x_, 2), core, y, x_ // 2)

    def mate(dz, dc):
        return (1 - zl if dz else zl), (1 - core if dc else core)

    def remote(src, dst, send, recv, target):
        return pltpu.make_async_remote_copy(
            src_ref=src, dst_ref=dst, send_sem=send, recv_sem=recv, device_id=target, device_id_type=MESH
        )

    barrier = pltpu.get_barrier_semaphore()

    def greet(target):
        pl.semaphore_signal(barrier, inc=1, device_id=target, device_id_type=MESH)

    for dz in (4, 3, 5, 2, 6):
        for dc in range(2):
            greet(device(lax.rem(z + dz, 8), xlo, (1 - core if dc else core), y, xhi))
    for d in range(1, 8):
        greet((outer, lax.rem(inner + d, 8)))
    for dz, dc in ((1, 0), (1, 1), (7, 0), (7, 1), (0, 1)):
        greet(device(lax.rem(z + dz, 8), xlo, (1 - core if dc else core), y, xhi))
    for dx in (1, 3):
        greet(across(lax.rem(x + dx, 4)))

    q_loads = [
        pltpu.make_async_copy(
            queries.at[:, :, pl.ds(g * 1024, 1024)], q_ref.at[g], loc.at[0, g]
        )
        for g in range(HK)
    ]
    g_loads = [
        pltpu.make_async_copy(
            out_grad.at[:, :, pl.ds(g * 1024, 1024)], g_ref.at[g], loc.at[1, g]
        )
        for g in range(HK)
    ]
    k_loads = [
        pltpu.make_async_copy(
            key_rows.at[:, :, pl.ds(g * HD, HD)], keys[g].at[pl.ds(inner * LB, LB)], loc.at[2, g]
        )
        for g in range(HK)
    ]
    def columns_a(blk, m):
        return inputs.at[:, pl.ds(pl.multiple_of(blk * 1024 + (m // 2) * 512 + (m % 2) * 128, 128), 128)]

    def columns_b(blk, c):
        return inputs.at[:, pl.ds(pl.multiple_of(blk * 1024 + 256 + c * 512, 256), 256)]

    x_loads = []
    for blk in range(8):
        x_loads += [
            pltpu.make_async_copy(columns_a(blk, member), xa_ref.at[blk, member], loc.at[3, blk]),
            pltpu.make_async_copy(columns_b(blk, core), xb_ref.at[blk, core], loc.at[4, blk]),
        ]
    choices = [
        pltpu.make_async_copy(sel_in, sel, loc.at[0, 4]),
        pltpu.make_async_copy(mask_in, mask, loc.at[0, 5]),
    ]
    for choice in choices:
        choice.start()
    for g in range(HK):
        k_loads[g].start()
        q_loads[g].start()
        g_loads[g].start()

    pl.semaphore_wait(barrier, 24)

    def key_copy(g, d):
        return remote(
            key_rows.at[:, :, pl.ds(g * HD, HD)],
            keys[g].at[pl.ds(inner * LB, LB)],
            key_s.at[g, d],
            key_r.at[g, d],
            (outer, lax.rem(inner + d, 8)),
        )

    def key_arrival(g, d):
        src = lax.rem(inner + 8 - d, 8)
        return remote(
            key_rows.at[:, :, pl.ds(g * HD, HD)],
            keys[g].at[pl.ds(src * LB, LB)],
            key_s.at[g, d],
            key_r.at[g, d],
            (outer, src),
        )

    def key_goes(d):
        return inner + d < 8

    def key_comes(d):
        return inner - d >= 0

    def send_keys(g):
        for d in range(1, 8):

            @pl.when(key_goes(d))
            def _():
                key_copy(g, d).start()

    send_keys(0)

    mates = [(0, 1), (1, 0), (1, 1)]

    def xa_copy(blk, dz, dc):
        pz, pc = mate(dz, dc)
        return remote(
            columns_a(blk, pz * 2 + pc),
            xa_ref.at[blk, member],
            xa_s.at[dz * 2 + dc, blk],
            xa_r.at[dz * 2 + dc, blk],
            device(zh * 2 + pz, xlo, pc, y, xhi),
        )

    def xa_arrival(blk, dz, dc):
        sz, sc = mate(dz, dc)
        return remote(
            columns_a(blk, member),
            xa_ref.at[blk, sz * 2 + sc],
            xa_s.at[dz * 2 + dc, blk],
            xa_r.at[dz * 2 + dc, blk],
            device(zh * 2 + sz, xlo, sc, y, xhi),
        )

    def xb_copy(blk):
        return remote(
            columns_b(blk, 1 - core),
            xb_ref.at[blk, core],
            xb_s.at[blk],
            xb_r.at[blk],
            device(z, xlo, 1 - core, y, xhi),
        )

    def xb_arrival(blk):
        return remote(
            columns_b(blk, core),
            xb_ref.at[blk, 1 - core],
            xb_s.at[blk],
            xb_r.at[blk],
            device(z, xlo, 1 - core, y, xhi),
        )

    for dz, dc in mates[::-1]:
        for blk in range(8):
            xa_copy(blk, dz, dc).start()
    for blk in range(8):
        xb_copy(blk).start()
    for load in x_loads:
        load.start()

    for choice in choices:
        choice.wait()

    for qb in range(LB):
        named = [jnp.where(mask[qb, s] == 1, sel[qb, s], -1) for s in range(SEL)]

        def invert(kb, carry):
            found = jnp.int32(SEL)
            for s in range(SEL):
                found = jnp.where(named[s] == kb, jnp.int32(s), found)
            inverse[qb, kb] = found
            return carry

        lax.fori_loop(0, inner * LB + LB, invert, 0)
    key_at = lax.broadcasted_iota(jnp.int32, (BLK, HD), 0)
    query_at = lax.rem(lax.broadcasted_iota(jnp.int32, (BLK, HD), 1), BLK)
    bias[0] = jnp.zeros((BLK, HD), jnp.float32)
    bias[1] = jnp.where(key_at <= query_at, 0.0, -1e30).astype(jnp.float32)
    bias[2] = jnp.full((BLK, HD), -1e30, jnp.float32)
    for qb in range(LB):
        contrib[qb, SEL] = jnp.zeros((BLK, HD), jnp.float32)

    def heads(ref, g, qb):
        return jnp.concatenate([ref[g, qb, :, pl.ds(h * HD, HD)] for h in range(GROUP)], axis=0)

    def attend(g):
        def one(qb, carry):
            place = inner * LB + qb
            query = heads(q_ref, g, qb)
            top = jnp.full((8, GROUP * BLK), -3e38, jnp.float32)
            for quad in range(4):
                picked, masks = [], []
                for s in range(4 * quad, 4 * quad + 4):
                    used = mask[qb, s] == 1
                    block = sel[qb, s]
                    picked.append(keys[g][jnp.where(used, block, place)])
                    kind = jnp.where(used, jnp.where(block == place, 1, 0), 2)
                    masks.append(bias[kind])
                scores = lax.dot_general(
                    jnp.concatenate(picked, axis=0),
                    query,
                    (((1,), (1,)), ((), ())),
                    preferred_element_type=jnp.float32,
                )
                shift = jnp.concatenate(masks, axis=0)
                scores = scores + jnp.concatenate([shift] * 4, axis=1)
                st_ref[quad] = scores
                top = jnp.maximum(top, jnp.max(scores.reshape(32, 8, GROUP * BLK), axis=0))
            top = jnp.max(top, axis=0, keepdims=True)
            total = jnp.zeros((8, GROUP * BLK), jnp.float32)
            for quad in range(4):
                weights = jnp.exp2((st_ref[quad] - top) * SCALE)
                st_ref[quad] = weights
                total = total + jnp.sum(weights.reshape(32, 8, GROUP * BLK), axis=0)
            norm = 1.0 / jnp.sum(total, axis=0, keepdims=True)
            grad = heads(g_ref, g, qb)
            for quad in range(4):
                probs = (st_ref[quad] * norm).astype(jnp.bfloat16)
                done = jnp.dot(probs, grad, preferred_element_type=jnp.float32)
                contrib[qb, pl.ds(4 * quad, 4)] = done.reshape(4, BLK, HD)
            return carry

        lax.fori_loop(0, LB, one, 0)

    def give_copy(g, j):
        d = inner - j
        return remote(
            give[g].at[j], came[g].at[d - 1], give_s.at[g, d], give_r.at[g, d], (outer, j)
        )

    def give_arrival(g, d):
        src = lax.rem(inner + d, 8)
        return remote(
            give[g].at[src], came[g].at[d - 1], give_s.at[g, d], give_r.at[g, d], (outer, src)
        )

    def terms_of(kb):
        terms = [contrib[qb, inverse[qb, kb]] for qb in range(LB)]
        return (terms[0] + terms[1]) + (terms[2] + terms[3])

    def hand_out(g):
        def owner(j, carry):
            for t in range(LB):
                give[g][j, t] = terms_of(j * LB + t).astype(jnp.bfloat16)
            give_copy(g, j).start()
            return carry

        lax.fori_loop(0, inner, owner, 0)
        for t in range(LB):
            vacc[g, t] = terms_of(inner * LB + t)

    def value_copy(g, dz, dc):
        pz, pc = mate(dz, dc)
        return remote(
            value[g].at[member],
            value[g].at[member],
            val_s.at[g, dz * 2 + dc],
            val_r.at[g, dz * 2 + dc],
            device(zh * 2 + pz, xlo, pc, y, xhi),
        )

    def value_arrival(g, dz, dc):
        sz, sc = mate(dz, dc)
        return remote(
            value[g].at[sz * 2 + sc],
            value[g].at[sz * 2 + sc],
            val_s.at[g, dz * 2 + dc],
            val_r.at[g, dz * 2 + dc],
            device(zh * 2 + sz, xlo, sc, y, xhi),
        )

    def own(g):
        for d in range(1, 8):

            @pl.when(inner + d < 8)
            def _():
                give_arrival(g, d).wait_recv()
                vacc[g] += came[g][d - 1].astype(jnp.float32)

        value[g][member] = vacc[g].reshape(LB * BLK, HD).astype(jnp.bfloat16)
        for dz, dc in mates[::-1]:
            value_copy(g, dz, dc).start()

    place_of = (y, x)

    def along(u, at_):
        return (outer, at_ * 2 + xhi) if u == 0 else across(at_)

    def part_copy(g, u, to):
        return remote(
            part[g].at[u, to],
            part_in[g].at[u, place_of[u]],
            p1_s.at[g, u * 4 + to],
            p1_r.at[g, u * 4 + place_of[u]],
            along(u, to),
        )

    def part_arrival(g, u, src):
        return remote(
            part[g].at[u, src],
            part_in[g].at[u, src],
            p1_s.at[g, u * 4 + src],
            p1_r.at[g, u * 4 + src],
            along(u, src),
        )

    def inputs_here():
        for load in x_loads:
            load.wait()
        for blk in range(8):
            xb_arrival(blk).wait_recv()
            for dz, dc in mates:
                xa_arrival(blk, dz, dc).wait_recv()

    def term_of(low_, wide):
        term = lax.dot_general(
            low_, wide, (((0,), (0,)), ((), ())), preferred_element_type=jnp.float32
        )
        return term.T.astype(jnp.bfloat16)

    def multiply(g):
        value_arrival(g, 0, 1).wait_recv()
        two = value[g][pl.ds(2 * zl, 2)].reshape(2 * LB * BLK, HD)
        for blk in range(8):
            to, hi = blk // 2, blk % 2
            rows = term_of(two, xb_ref[blk].reshape(2 * LB * BLK, 256))
            rows = rows.reshape(2, 2, 2, 32, HD)
            for lo in range(2):
                part[g][0, to, 2 * hi + lo, pl.ds(0, 2)] = rows[0, lo]
                part[g][1, 2 * hi + lo, to, pl.ds(0, 2)] = rows[1, lo]
        for dc in range(2):
            value_arrival(g, 1, dc).wait_recv()
        four = value[g][...].reshape(4 * LB * BLK, HD)
        for to in range(4):
            wide = jnp.concatenate([xa_ref[2 * to], xa_ref[2 * to + 1]], axis=-1)
            rows = term_of(four, wide.reshape(4 * LB * BLK, 256)).reshape(4, 2, 32, HD)
            part[g][0, to, :, 2] = rows[:, 0]
            for at_ in range(4):
                part[g][1, at_, to, 2] = rows[at_, 1]
            send_part(g, 0, to)
        for to in range(4):
            send_part(g, 1, to)

    def send_part(g, u, to):
        @pl.when(place_of[u] != to)
        def _():
            part_copy(g, u, to).start()

        @pl.when(place_of[u] == to)
        def _():
            part_in[g][u, to] = part[g][u, to]

    def mid_copy(g, u, d):
        to = lax.rem(place_of[1 - u] + d, 4)
        return remote(
            mid[g].at[u, to],
            mid_in[g].at[u, d],
            p2_s.at[g, u * 4 + d],
            p2_r.at[g, u * 4 + d],
            along(1 - u, to),
        )

    def mid_arrival(g, u, d):
        src = lax.rem(place_of[1 - u] + 4 - d, 4)
        return remote(
            mid[g].at[u, src],
            mid_in[g].at[u, d],
            p2_s.at[g, u * 4 + d],
            p2_r.at[g, u * 4 + d],
            along(1 - u, src),
        )

    def sum_first(g):
        for u in range(2):
            for src in range(4):

                @pl.when(place_of[u] != src)
                def _():
                    part_arrival(g, u, src).wait_recv()

            terms = [part_in[g][u, k].astype(jnp.float32) for k in range(4)]
            total = (terms[0] + terms[1]) + (terms[2] + terms[3])
            mid[g][u] = total.astype(MID)
            for d in range(1, 4):
                mid_copy(g, u, d).start()

    def low_target(u, k):
        return (4 * zl + core, u) if k == 2 else (4 * core + 2 + u, k)

    def low_copy(g, u, k):
        to_z, to_core = low_target(u, k)
        return remote(
            low[g].at[u, k],
            low_in[g].at[z],
            p3_s.at[g, u * 3 + k],
            p3_r.at[g, z],
            device(to_z, xlo, to_core, y, xhi),
        )

    def low_stays(u, k):
        to_z, to_core = low_target(u, k)
        return (to_z == z) & (to_core == core)

    wide_z = lax.rem(z, 4) >= 2
    from_core = jnp.where(wide_z, z // 4, lax.rem(z, 2))

    def low_comes(src):
        return wide_z | (src % 2 == z // 4)

    def low_is_own(src):
        return (src == z) & (from_core == core)

    def low_arrival(g, src):
        return remote(
            low[g].at[0, 0],
            low_in[g].at[src],
            p3_s.at[g, 0],
            p3_r.at[g, src],
            device(src, xlo, from_core, y, xhi),
        )

    def sum_second(g):
        for u in range(2):
            total = mid[g][u, place_of[1 - u]].astype(jnp.float32)
            for d in range(1, 4):
                mid_arrival(g, u, d).wait_recv()
                total = total + mid_in[g][u, d].astype(jnp.float32)
            low[g][u] = total.astype(MID)
            for k in range(3):

                @pl.when(jnp.logical_not(low_stays(u, k)))
                def _():
                    low_copy(g, u, k).start()

                @pl.when(low_stays(u, k))
                def _():
                    low_in[g][z] = low[g][u, k]

    def sum_z(g):
        column = pl.ds(g * HD, HD)
        out_ref[:, column] = jnp.zeros((32, HD), jnp.float32)
        for src in range(8):

            @pl.when(low_comes(src) & jnp.logical_not(low_is_own(src)))
            def _():
                low_arrival(g, src).wait_recv()

            @pl.when(low_comes(src))
            def _():
                out_ref[:, column] += low_in[g][src].astype(jnp.float32)

    def start_of(g):
        for d in range(1, 8):

            @pl.when(key_comes(d))
            def _():
                key_arrival(g, d).wait_recv()

        k_loads[g].wait()
        q_loads[g].wait()
        g_loads[g].wait()

    def next_keys(g):
        for d in range(1, 8):

            @pl.when(key_goes(d))
            def _():
                key_copy(g - 1, d).wait_send()
                key_copy(g, d).start()

    def step(g):
        start_of(g)
        attend(g)
        hand_out(g)
        if g + 2 < HK:
            next_keys(g + 2)

    next_keys(1)
    def early_left(g):
        for d in range(1, 8):
            if g + 1 == HK:

                @pl.when(key_goes(d))
                def _():
                    key_copy(g, d).wait_send()

            @pl.when(inner - d >= 0)
            def _():
                give_copy(g, inner - d).wait_send()

        for dz, dc in mates:
            value_copy(g, dz, dc).wait_send()

    def inputs_left():
        for blk in range(8):
            xb_copy(blk).wait_send()
            for dz, dc in mates:
                xa_copy(blk, dz, dc).wait_send()

    def sums_left(g):
        for u in range(2):
            for to in range(4):

                @pl.when(place_of[u] != to)
                def _():
                    part_copy(g, u, to).wait_send()

            for d in range(1, 4):
                mid_copy(g, u, d).wait_send()

    def low_left(g):
        for u in range(2):
            for k in range(3):

                @pl.when(jnp.logical_not(low_stays(u, k)))
                def _():
                    low_copy(g, u, k).wait_send()

    step(0)
    step(1)
    own(0)
    step(2)
    own(1)
    step(3)
    inputs_here()
    multiply(0)
    multiply(1)
    own(2)
    sum_first(0)
    own(3)
    inputs_left()
    multiply(2)
    sum_first(1)
    sum_second(0)
    multiply(3)
    sum_first(2)
    sum_second(1)
    for g in range(HK):
        early_left(g)
    sum_first(3)
    sum_second(2)
    for g in range(3):
        sums_left(g)
    sum_z(0)
    sum_z(1)
    sum_second(3)
    sums_left(3)
    sum_z(2)
    for g in range(3):
        low_left(g)
    sum_z(3)
    low_left(3)


def body(inputs, queries, key_rows, out_grad, sel_blocks, block_mask):
    any_ref = pl.BlockSpec(memory_space=pl.ANY)
    bf16, f32 = jnp.bfloat16, jnp.float32
    dma = pltpu.SemaphoreType.DMA
    scratch = (
        [pltpu.VMEM((NB, BLK, HD), bf16)] * HK
        + [pltpu.VMEM((8, LB, BLK, HD), bf16)] * HK
        + [pltpu.VMEM((7, LB, BLK, HD), bf16)] * HK
        + [pltpu.VMEM((4, LB * BLK, HD), bf16)] * HK
        + [pltpu.VMEM((2, 4, 4, 3, 32, HD), bf16)] * HK
        + [pltpu.VMEM((2, 4, 4, 3, 32, HD), bf16)] * HK
        + [pltpu.VMEM((2, 4, 3, 32, HD), MID)] * HK
        + [pltpu.VMEM((2, 4, 3, 32, HD), MID)] * HK
        + [pltpu.VMEM((2, 3, 32, HD), MID)] * HK
        + [pltpu.VMEM((8, 32, HD), MID)] * HK
        + [
            pltpu.VMEM((HK, LB, BLK, 1024), bf16),
            pltpu.VMEM((HK, LB, BLK, 1024), bf16),
            pltpu.VMEM((8, 4, LB * BLK, 128), bf16),
            pltpu.VMEM((8, 2, LB * BLK, 256), bf16),
            pltpu.VMEM((4, 256, GROUP * BLK), f32),
            pltpu.VMEM((LB, SEL + 1, BLK, HD), f32),
            pltpu.VMEM((3, BLK, HD), f32),
            pltpu.VMEM((HK, LB, BLK, HD), f32),
            pltpu.SMEM((LB, NB), jnp.int32),
            pltpu.SMEM((LB, SEL), jnp.int32),
            pltpu.SMEM((LB, SEL), jnp.int32),
        ]
        + [
            dma((5, 8)),
            dma((HK, 8)),
            dma((HK, 8)),
            dma((4, 8)),
            dma((4, 8)),
            dma((8,)),
            dma((8,)),
            dma((HK, 8)),
            dma((HK, 8)),
            dma((HK, 4)),
            dma((HK, 4)),
        ]
        + [dma((HK, 8))] * 6
    )
    return pl.pallas_call(
        kernel,
        out_shape=jax.ShapeDtypeStruct((32, HK * HD), f32),
        in_specs=[any_ref] * 6,
        out_specs=pl.BlockSpec(memory_space=pltpu.VMEM),
        scratch_shapes=scratch,
        compiler_params=pltpu.CompilerParams(
            collective_id=0, has_side_effects=True, vmem_limit_bytes=56 * 1024 * 1024
        ),
        cost_estimate=pl.CostEstimate(
            flops=6_500_000_000, bytes_accessed=9_000_000, transcendentals=8_400_000
        ),
    )(
        inputs,
        queries.reshape(LB, BLK, 4096),
        key_rows.reshape(LB, BLK, 512),
        out_grad.reshape(LB, BLK, 4096),
        sel_blocks,
        block_mask,
    )


def solution(mesh):
    placed = P(("outer", "inner"), None)
    return jax.shard_map(
        body, mesh=mesh, in_specs=(placed,) * 6, out_specs=P(("inner", "outer"), None), check_vma=False
    )
```
